32 devices in a mesh: groups: 2 (over x), gx: 16 (over z, y, core).
Axes of the slice: x: 2, y: 2, z: 4, core: 2. Of those that a mesh axis runs over, the one named last changes fastest.
Arguments:
- activations: bfloat16 [1024, 18432], P('groups', 'gx'), parts along dimension 0, may hold values from -25 to 25, as said below
- norm_gain: float32 [18432], P('gx'), may hold values from 0.1 to 1.9
- w_up: bfloat16 [18432, 8192], P('gx'), may hold values from -0.0625 to 0.0625
- w_down: bfloat16 [8192, 18432], P(None, 'gx'), may hold values from -0.0625 to 0.0625
Outputs:
- layer_out: bfloat16 [1024, 18432], P('groups', 'gx'), parts along dimension 0
The draws below stay inside these ranges and needn't reach their ends.
There are 2 independent parts, one for each index of `groups`. The reference program is written for one: setup_inputs(seed, part) draws one part's arguments, and reference() takes and returns one part's arrays. A program takes and returns all parts, laid end to end along the dimension named above; an argument that names none is the same for every part. Nothing has to cross between parts.
Inputs may be any that keep to these rules, and one draw needn't show every extreme that they name: Every batch row of activations has a root-mean-square over the features of at least 0.1.
All inputs are finite; a program needn't handle non-finite values.
Results may differ from the reference program's by a relative error of at most 0.0043.
Values may be sent and summed in bfloat16 or wider, within the bound.
A program may use at most 128 MiB of HBM per device.

```python
import math
import jax
import jax.numpy as jnp
from jax import lax

D = 18432
HID = 8192
B = 512


def draw_activations(key, part):
    key = jax.random.fold_in(key, 11)
    key_base = jax.random.fold_in(key, 1)
    key_cols = jax.random.fold_in(key, 2)
    key_rows = jax.random.fold_in(key, 3)
    ramp = 0.6 * jnp.power(3.0, jnp.arange(D, dtype=jnp.float32) / (D - 1))
    base = jnp.clip(jax.random.normal(key_base, (B, D), jnp.float32), -4.0, 4.0)
    rough = jnp.exp(jax.random.uniform(key_cols, (D,), jnp.float32, -0.3, 0.3))
    row_mult = jnp.exp(jax.random.uniform(key_rows, (B, 1), jnp.float32, math.log(0.7), math.log(1.4)))
    values = base * (ramp * rough)[None, :] * row_mult
    return values.astype(jnp.bfloat16)


def raised(values, rng, source, target, parts, factor):
    owner, partner = [(jnp.arange(values.shape[axis_at]) // (values.shape[axis_at] // parts)).reshape([-1 if axis == axis_at else 1 for axis in range(values.ndim)]) for axis_at in (source, target)]
    chosen = jax.random.permutation(rng, parts)[partner]
    strong = (owner == chosen) | (owner == (partner + parts // 2) % parts)
    return jnp.where(strong, factor * values, values)


def level_of(key, dims, shards, smallest, top_value):
    factor_of = 1.0
    for dim, shards_of in shards:
        draws = jax.random.uniform(jax.random.fold_in(jax.random.fold_in(key, 6), dim), (shards_of,), jnp.float32, smallest / len(shards), top_value / len(shards))
        factor_of = factor_of * jnp.repeat(jnp.exp(draws), dims[dim] // shards_of).reshape((-1,) + (1,) * (len(dims) - 1 - dim))
    return factor_of


def scatter_about(key, shape, spread, bound, split=(), kind=jnp.bfloat16):
    values = jax.random.normal(key, shape, jnp.float32) * spread
    if len(split) > 0:
        values = level_of(key, shape, split, -0.22, 0.18) * values
    return jnp.clip(values, min=-bound, max=bound).astype(kind)


def bell_draw_with(own_key, shape, spread, reach, shards, heavy, kind=jnp.bfloat16):
    drawn = spread * jax.random.normal(own_key, shape, jnp.float32)
    if shards:
        drawn = drawn * level_of(own_key, shape, shards, -0.22, 0.18)
    return jnp.clip(raised(drawn, jax.random.fold_in(own_key, 3), *heavy), -reach, reach).astype(kind)


def setup_inputs(seed: int = 0, part: int = 0) -> dict:
    streams_of = jax.random.split(jax.random.key(seed), 5)
    part_splits = jax.random.split(jax.random.fold_in(streams_of[4], part), 5)
    activations = draw_activations(jax.random.fold_in(jax.random.fold_in(streams_of[4], part), 71), part)
    norm_gain = jnp.clip(1.0 + 0.18 * jax.random.normal(streams_of[1], (D,), jnp.float32), 0.1, 1.9)
    w_up = bell_draw_with(streams_of[2], (D, HID), D ** -0.5, 0.0625, ((0, 16),), (0, 1, 16, 2.0))
    w_down = scatter_about(streams_of[3], (HID, D), HID ** -0.5, 0.0625, ((1, 16),))
    return {"activations": activations, "norm_gain": norm_gain, "w_up": w_up, "w_down": w_down}


def reference(activations, norm_gain, w_up, w_down):
    wide_act = activations.astype(jnp.float32)
    squares = lax.optimization_barrier(jnp.sum(wide_act * wide_act, axis=1))
    row_scale = lax.rsqrt(squares / D + 1e-06)
    normed = (wide_act * norm_gain[None, :]).astype(jnp.bfloat16)
    pre = jnp.dot(normed, w_up, preferred_element_type=jnp.float32) * row_scale[:, None]
    hidden = jax.nn.gelu(pre, approximate=False).astype(jnp.bfloat16)
    down_sum = jnp.dot(hidden, w_down, preferred_element_type=jnp.float32)
    return (wide_act + down_sum).astype(jnp.bfloat16)
```

```python
import functools

import jax
import jax.numpy as jnp
from jax import lax
from jax.experimental import pallas as pl
from jax.experimental.pallas import tpu as pltpu
from jax.sharding import PartitionSpec as P

CHUNK = 1024
MESH = pl.DeviceIdType.MESH


def kernel(dims, act, gain, wup, wdn, out, *scratch):
    n, depth, width, chunks = dims
    (normed, acc, scale, wub, wdb, keep0, keep1, keep2, s_core, r_core, s_y, r_y, s_z, r_z, gath, sq_s, sq_r, sq_z,
     wu_sem, wd_sem, cs, cr, ys, yr, zs, zr, ags, agr, ays, ayr, acs, acr, qs, qr, qzs, qzr) = scratch
    batch = act.shape[0]
    half = CHUNK // 2
    rows = batch // 2
    nz = n // 4
    block = rows // nz

    me = lax.axis_index("gx")
    core = lax.rem(me, 2)
    y = lax.rem(me // 2, 2)
    z = me // 4
    core_peer = me + 1 - 2 * core
    y_peer = me + 2 - 4 * y
    z_others = [lax.rem(z + j, nz) for j in range(1, nz)]

    def z_peer(other):
        return other * 4 + y * 2 + core

    def rdma(src, dst, send, recv, peer):
        return pltpu.make_async_remote_copy(
            src_ref=src, dst_ref=dst, send_sem=send, recv_sem=recv, device_id={"gx": peer}, device_id_type=MESH
        )

    def up_copies(c, slot):
        return [
            pltpu.make_async_copy(
                wup.at[:, pl.ds(pl.multiple_of(c * CHUNK + which * half, half), half)], wub.at[slot, k], wu_sem.at[slot, k]
            )
            for k, which in enumerate((1 - core, core))
        ]

    def down_copy(c, slot):
        return pltpu.make_async_copy(
            wdn.at[pl.ds(pl.multiple_of(c * CHUNK, CHUNK), CHUNK), :], wdb.at[slot], wd_sem.at[slot]
        )

    def core_rs(c):
        return rdma(s_core.at[c], r_core.at[c], cs.at[c], cr.at[c], core_peer)

    def y_rs(c):
        return rdma(s_y.at[c], r_y.at[c], ys.at[c], yr.at[c], y_peer)

    def z_rs_to(c, o):
        return rdma(
            s_z.at[c, pl.ds(pl.multiple_of(o * block, block), block)], r_z.at[c, z], zs.at[c, o], zr.at[c, z], z_peer(o)
        )

    def z_rs_from(c, o):
        return rdma(
            s_z.at[c, pl.ds(pl.multiple_of(o * block, block), block)], r_z.at[c, o], zs.at[c, o], zr.at[c, o], z_peer(o)
        )

    def z_rows(o):
        return pl.ds(pl.multiple_of(y * rows + o * block, block), block)

    def z_ag_to(c, o):
        part = gath.at[c, core, z_rows(z)]
        return rdma(part, part, ags.at[c, o], agr.at[c, z], z_peer(o))

    def z_ag_from(c, o):
        part = gath.at[c, core, z_rows(o)]
        return rdma(part, part, ags.at[c, o], agr.at[c, o], z_peer(o))

    def y_part(c, which):
        part = gath.at[c, core, pl.ds(pl.multiple_of(which * rows, rows), rows)]
        return rdma(part, part, ays.at[c], ayr.at[c], y_peer)

    def core_part(c, which):
        part = gath.at[c, which]
        return rdma(part, part, acs.at[c], acr.at[c], core_peer)

    def sq_core():
        return rdma(sq_s.at[0], sq_r.at[0], qs.at[0], qr.at[0], core_peer)

    def sq_y():
        return rdma(sq_s.at[1], sq_r.at[1], qs.at[1], qr.at[1], y_peer)

    def sq_to(o):
        return rdma(sq_s.at[2], sq_z.at[z], qzs.at[o], qzr.at[z], z_peer(o))

    def sq_from(o):
        return rdma(sq_s.at[2], sq_z.at[o], qzs.at[o], qzr.at[o], z_peer(o))

    for slot in range(2):
        for copy in up_copies(slot, slot):
            copy.start()
        down_copy(slot, slot).start()

    barrier = pltpu.get_barrier_semaphore()
    peers = [core_peer, y_peer] + [z_peer(o) for o in z_others]
    for peer in peers:
        pl.semaphore_signal(barrier, inc=1, device_id={"gx": peer}, device_id_type=MESH)

    wide = act[...].astype(jnp.float32)
    normed[...] = (wide * gain[...]).astype(jnp.bfloat16)
    acc[...] = wide
    squares = jnp.broadcast_to(jnp.sum(wide * wide, axis=1, keepdims=True), (batch, 128))
    sq_s[0] = squares.T[:8]

    pl.semaphore_wait(barrier, len(peers))
    sq_core().start()

    def up(c):
        slot = lax.rem(c, 2)
        for copy in up_copies(c, slot):
            copy.wait()
        s_core[c] = jnp.dot(normed[...], wub[slot, 0], preferred_element_type=jnp.float32).astype(jnp.bfloat16)
        core_rs(c).start()
        keep0[slot] = jnp.dot(normed[...], wub[slot, 1], preferred_element_type=jnp.float32)

        @pl.when(c + 2 < chunks)
        def _():
            for copy in up_copies(c + 2, slot):
                copy.start()

    def sum_core(c):
        slot = lax.rem(c, 2)
        core_rs(c).wait_recv()
        theirs = pl.ds(pl.multiple_of((1 - y) * rows, rows), rows)
        mine = pl.ds(pl.multiple_of(y * rows, rows), rows)
        s_y[c] = (keep0[slot, theirs] + r_core[c, theirs].astype(jnp.float32)).astype(jnp.bfloat16)
        y_rs(c).start()
        keep1[slot] = keep0[slot, mine] + r_core[c, mine].astype(jnp.float32)

    def sum_y(c):
        slot = lax.rem(c, 2)
        y_rs(c).wait_recv()
        s_z[c] = (keep1[slot] + r_y[c].astype(jnp.float32)).astype(jnp.bfloat16)
        for o in z_others:
            z_rs_to(c, o).start()
        mine = pl.ds(pl.multiple_of(z * block, block), block)
        keep2[slot] = keep1[slot, mine] + r_y[c, mine].astype(jnp.float32)

    def sum_z(c):
        slot = lax.rem(c, 2)
        total = keep2[slot]
        for o in z_others:
            z_rs_from(c, o).wait_recv()
            total = total + r_z[c, o].astype(jnp.float32)
        pre = total * scale[z_rows(z), :][:, :1]
        hidden = 0.5 * pre * (1.0 + lax.erf(pre * 0.7071067811865476))
        gath[c, core, z_rows(z)] = hidden.astype(jnp.bfloat16)
        for o in z_others:
            z_ag_to(c, o).start()

    def gather_z(c):
        for o in z_others:
            z_ag_from(c, o).wait_recv()
        y_part(c, y).start()

    def gather_y(c):
        y_part(c, 1 - y).wait_recv()
        core_part(c, core).start()

    def down(c):
        slot = lax.rem(c, 2)
        down_copy(c, slot).wait()
        core_part(c, 1 - core).wait_recv()
        acc[...] += jnp.dot(gath[c, 0], wdb[slot, :half], preferred_element_type=jnp.float32)
        acc[...] += jnp.dot(gath[c, 1], wdb[slot, half:], preferred_element_type=jnp.float32)

        @pl.when(c + 2 < chunks)
        def _():
            down_copy(c + 2, slot).start()

    stages = [(5, gather_y), (4, gather_z), (3, sum_z), (2, sum_y), (1, sum_core), (0, up), (6, down)]

    def step(t, carry):
        @pl.when(t == 1)
        def _():
            sq_core().wait_recv()
            sq_s[1] = sq_s[0] + sq_r[0]
            sq_y().start()

        @pl.when(t == 2)
        def _():
            sq_y().wait_recv()
            sq_s[2] = sq_s[1] + sq_r[1]
            for o in z_others:
                sq_to(o).start()

        @pl.when(t == 3)
        def _():
            total = sq_s[2]
            for o in z_others:
                sq_from(o).wait_recv()
                total = total + sq_z[o]
            row_scale = lax.rsqrt(total / (depth * n) + 1e-06)
            scale[...] = jnp.broadcast_to(row_scale[:1], (128, batch)).T

        for offset, stage in stages:
            c = t - offset

            @pl.when(jnp.logical_and(c >= 0, c < chunks))
            def _(c=c, stage=stage):
                stage(c)

        return carry

    lax.fori_loop(0, chunks + 6, step, 0)

    out[...] = acc[...].astype(jnp.bfloat16)

    sq_core().wait_send()
    sq_y().wait_send()
    for o in z_others:
        sq_to(o).wait_send()

    def drain(c, carry):
        core_rs(c).wait_send()
        y_rs(c).wait_send()
        for o in z_others:
            z_rs_to(c, o).wait_send()
            z_ag_to(c, o).wait_send()
        y_part(c, y).wait_send()
        core_part(c, core).wait_send()
        return carry

    lax.fori_loop(0, chunks, drain, 0)


def local(n, activations, norm_gain, w_up, w_down):
    batch, depth = activations.shape
    width = w_up.shape[1]
    chunks = width // CHUNK
    half, rows, nz = CHUNK // 2, batch // 2, n // 4
    block = rows // nz
    bf16, f32 = jnp.bfloat16, jnp.float32
    vmem, dma = pltpu.VMEM, pltpu.SemaphoreType.DMA
    in_vmem = pl.BlockSpec(memory_space=pltpu.VMEM)
    in_hbm = pl.BlockSpec(memory_space=pl.ANY)
    return pl.pallas_call(
        functools.partial(kernel, (n, depth, width, chunks)),
        out_shape=jax.ShapeDtypeStruct((batch, depth), bf16),
        in_specs=[in_vmem, in_vmem, in_hbm, in_hbm],
        out_specs=in_vmem,
        scratch_shapes=[
            vmem((batch, depth), bf16),
            vmem((batch, depth), f32),
            vmem((batch, 128), f32),
            vmem((2, 2, depth, half), bf16),
            vmem((2, CHUNK, depth), bf16),
            vmem((2, batch, half), f32),
            vmem((2, rows, half), f32),
            vmem((2, block, half), f32),
            vmem((chunks, batch, half), bf16),
            vmem((chunks, batch, half), bf16),
            vmem((chunks, rows, half), bf16),
            vmem((chunks, rows, half), bf16),
            vmem((chunks, rows, half), bf16),
            vmem((chunks, nz, block, half), bf16),
            vmem((chunks, 2, batch, half), bf16),
            vmem((3, 8, batch), f32),
            vmem((2, 8, batch), f32),
            vmem((nz, 8, batch), f32),
            dma((2, 2)),
            dma((2,)),
            dma((chunks,)),
            dma((chunks,)),
            dma((chunks,)),
            dma((chunks,)),
            dma((chunks, nz)),
            dma((chunks, nz)),
            dma((chunks, nz)),
            dma((chunks, nz)),
            dma((chunks,)),
            dma((chunks,)),
            dma((chunks,)),
            dma((chunks,)),
            dma((2,)),
            dma((2,)),
            dma((nz,)),
            dma((nz,)),
        ],
        compiler_params=pltpu.CompilerParams(
            collective_id=0, has_side_effects=True, vmem_limit_bytes=60 * 1024 * 1024
        ),
        cost_estimate=pl.CostEstimate(
            flops=4 * batch * depth * width, bytes_accessed=4 * depth * width, transcendentals=batch * width // n
        ),
    )(activations, norm_gain[None, :], w_up, w_down)


def solution(mesh):
    return jax.shard_map(
        functools.partial(local, mesh.shape["gx"]),
        mesh=mesh,
        in_specs=(P("groups", "gx"), P("gx"), P("gx", None), P(None, "gx")),
        out_specs=P("groups", "gx"),
        check_vma=False,
    )
```

```python
import functools

import jax
import jax.numpy as jnp
from jax import lax
from jax.experimental import pallas as pl
from jax.experimental.pallas import tpu as pltpu
from jax.sharding import PartitionSpec as P

CHUNK = 512
EVERY = 4
LAST = 14
MESH = pl.DeviceIdType.MESH


def kernel(dims, act, gain, wup, wdn, out, *scratch):
    n, depth, width, chunks = dims
    (normed, acc, scale, wub, wdb, keep, s_core, r_core, s_y, r_y, s_z, r_z, s_m, r_m, gath, sq_s, sq_r, sq_z,
     wu_sem, wd_sem, cs, cr, ys, yr, zs, zr, ags, agr, ays, ayr, acs, acr, qs, qr, qzs, qzr) = scratch
    batch = act.shape[0]
    half = CHUNK // 2
    nz = n // 4

    me = lax.axis_index("gx")
    core = lax.rem(me, 2)
    y = lax.rem(me // 2, 2)
    z = me // 4
    core_peer = me + 1 - 2 * core
    y_peer = me + 2 - 4 * y
    z_others = [lax.rem(z + j, nz) for j in range(1, nz)]

    def z_peer(other):
        return other * 4 + y * 2 + core

    tree = nz == 4
    pair = z // 2
    near = z + 1 - 2 * lax.rem(z, 2)
    far = (2 - pair, 3 - 3 * pair)
    at_end = jnp.logical_or(z == 0, z == nz - 1)
    in_middle = jnp.logical_not(at_end)

    def rdma(src, dst, send, recv, peer):
        return pltpu.make_async_remote_copy(
            src_ref=src, dst_ref=dst, send_sem=send, recv_sem=recv, device_id={"gx": peer}, device_id_type=MESH
        )

    def up_copies(c, slot):
        return [
            pltpu.make_async_copy(
                wup.at[:, pl.ds(pl.multiple_of(c * CHUNK + which * half, half), half)], wub.at[slot, k], wu_sem.at[slot, k]
            )
            for k, which in enumerate((1 - core, core))
        ]

    def down_copy(c, slot):
        return pltpu.make_async_copy(
            wdn.at[pl.ds(pl.multiple_of(c * CHUNK, CHUNK), CHUNK), :], wdb.at[slot], wd_sem.at[slot]
        )

    def core_rs(c):
        return rdma(s_core.at[c], r_core.at[c], cs.at[c], cr.at[c], core_peer)

    def area(start, size):
        return pl.ds(pl.multiple_of(start, 16), size)

    def shape_of(z_first):
        if z_first:
            z_len = batch // nz
            return 0, z_len, z * z_len, z_len // 2
        y_len = batch // 2
        return y * y_len, y_len // nz, 0, y_len

    def y_rs(zf, c):
        y_len = shape_of(zf)[3]
        return rdma(s_y.at[c, pl.ds(0, y_len)], r_y.at[c, pl.ds(0, y_len)], ys.at[c], yr.at[c], y_peer)

    def z_end(zf, c):
        z_len = shape_of(zf)[1]
        three = area((1 - pair) * z_len, 3 * z_len)
        return rdma(s_z.at[c, three], r_z.at[c, three], zs.at[c, 0], zr.at[c, 0], z_peer(near))

    def z_mid(zf, c):
        z_len = shape_of(zf)[1]
        return rdma(
            s_z.at[c, area(near * z_len, z_len)], r_m.at[c, 0, pl.ds(0, z_len)], zs.at[c, 0], zr.at[c, 0], z_peer(near)
        )

    def z_merged(zf, c, j):
        z_len = shape_of(zf)[1]
        return rdma(
            s_m.at[c, j, pl.ds(0, z_len)], r_m.at[c, 1, pl.ds(0, z_len)], zs.at[c, 1 + j], zr.at[c, 1], z_peer(far[j])
        )

    def z_direct(zf, c, o, slot):
        z_len = shape_of(zf)[1]
        return rdma(s_z.at[c, area(o * z_len, z_len)], r_z.at[c, area(slot * z_len, z_len)], zs.at[c, o], zr.at[c, slot], z_peer(o))

    def z_part(zf, c, o):
        base, z_len = shape_of(zf)[:2]
        return gath.at[c, core, area(base + o * z_len, z_len)]

    def g_near(zf, c, o):
        return rdma(z_part(zf, c, o), z_part(zf, c, o), ags.at[c, 0], agr.at[c, 0], z_peer(near))

    def g_far(zf, c, o, slot):
        return rdma(z_part(zf, c, o), z_part(zf, c, o), ags.at[c, 1], agr.at[c, slot], z_peer(far[0]))

    def g_two(zf, c):
        base, z_len = shape_of(zf)[:2]
        part = gath.at[c, core, area(base + (1 - pair) * 2 * z_len, 2 * z_len)]
        return rdma(part, part, ags.at[c, 2], agr.at[c, 1], z_peer(near))

    def g_direct(zf, c, o, slot):
        return rdma(z_part(zf, c, slot), z_part(zf, c, slot), ags.at[c, o], agr.at[c, slot], z_peer(o))

    def y_part(zf, c, which):
        base, y_len = shape_of(zf)[2:]
        part = gath.at[c, core, area(base + which * y_len, y_len)]
        return rdma(part, part, ays.at[c], ayr.at[c], y_peer)

    def core_part(c, which):
        part = gath.at[c, which]
        return rdma(part, part, acs.at[c], acr.at[c], core_peer)

    def sq_core():
        return rdma(sq_s.at[0], sq_r.at[0], qs.at[0], qr.at[0], core_peer)

    def sq_y():
        return rdma(sq_s.at[1], sq_r.at[1], qs.at[1], qr.at[1], y_peer)

    def sq_to(o):
        return rdma(sq_s.at[2], sq_z.at[z], qzs.at[o], qzr.at[z], z_peer(o))

    def sq_from(o):
        return rdma(sq_s.at[2], sq_z.at[o], qzs.at[o], qzr.at[o], z_peer(o))

    for slot in range(2):
        for copy in up_copies(slot, slot):
            copy.start()
        down_copy(slot, slot).start()

    barrier = pltpu.get_barrier_semaphore()
    peers = [core_peer, y_peer] + [z_peer(o) for o in z_others]
    for peer in peers:
        pl.semaphore_signal(barrier, inc=1, device_id={"gx": peer}, device_id_type=MESH)

    wide = act[...].astype(jnp.float32)
    normed[...] = (wide * gain[...]).astype(jnp.bfloat16)
    acc[...] = wide
    squares = jnp.broadcast_to(jnp.sum(wide * wide, axis=1, keepdims=True), (batch, 128))
    sq_s[0] = squares.T[:8]

    pl.semaphore_wait(barrier, len(peers))
    sq_core().start()

    def up(c):
        slot = lax.rem(c, 2)
        for copy in up_copies(c, slot):
            copy.wait()
        s_core[c] = jnp.dot(normed[...], wub[slot, 0], preferred_element_type=jnp.float32).astype(jnp.bfloat16)
        core_rs(c).start()
        keep[c] = jnp.dot(normed[...], wub[slot, 1], preferred_element_type=jnp.float32)

        @pl.when(c + 2 < chunks)
        def _():
            for copy in up_copies(c + 2, slot):
                copy.start()

    def send_y(zf, c):
        base, y_len = shape_of(zf)[2:]
        s_y[c, :y_len] = keep[c, area(base + (1 - y) * y_len, y_len)].astype(jnp.bfloat16)
        y_rs(zf, c).start()

    def take_y(zf, c):
        base, y_len = shape_of(zf)[2:]
        y_rs(zf, c).wait_recv()
        keep[c, area(base + y * y_len, y_len)] += r_y[c, :y_len].astype(jnp.float32)

    def send_z(zf, c):
        base, z_len = shape_of(zf)[:2]
        s_z[c, : nz * z_len] = keep[c, area(base, nz * z_len)].astype(jnp.bfloat16)
        if not tree:
            for o in z_others:
                z_direct(zf, c, o, z).start()
            return

        @pl.when(at_end)
        def _():
            z_end(zf, c).start()

        @pl.when(in_middle)
        def _():
            z_mid(zf, c).start()

    def merge_z(zf, c):
        base, z_len = shape_of(zf)[:2]
        if not tree:
            return

        @pl.when(in_middle)
        def _():
            z_end(zf, c).wait_recv()
            for j in range(2):
                mine = keep[c, area(base + far[j] * z_len, z_len)]
                theirs = r_z[c, area(far[j] * z_len, z_len)].astype(jnp.float32)
                s_m[c, j, :z_len] = (mine + theirs).astype(jnp.bfloat16)
                z_merged(zf, c, j).start()
            keep[c, area(base + z * z_len, z_len)] += r_z[c, area(z * z_len, z_len)].astype(jnp.float32)

    def take_z(zf, c):
        base, z_len = shape_of(zf)[:2]
        own = area(base + z * z_len, z_len)
        if not tree:
            for o in z_others:
                z_direct(zf, c, o, o).wait_recv()
                keep[c, own] += r_z[c, area(o * z_len, z_len)].astype(jnp.float32)
            return

        @pl.when(at_end)
        def _():
            z_mid(zf, c).wait_recv()
            keep[c, own] += r_m[c, 0, :z_len].astype(jnp.float32)

        z_merged(zf, c, 0).wait_recv()
        keep[c, own] += r_m[c, 1, :z_len].astype(jnp.float32)

    def activate(zf, c):
        z_base, z_len, y_base, y_len = shape_of(zf)
        own = area(y_base + y * y_len, y_len) if zf else area(z_base + z * z_len, z_len)
        pre = keep[c, own] * scale[own, :][:, :1]
        hidden = 0.5 * pre * (1.0 + lax.erf(pre * 0.7071067811865476))
        gath[c, core, own] = hidden.astype(jnp.bfloat16)

    def spread_z(zf, c):
        if not tree:
            for o in z_others:
                g_direct(zf, c, o, z).start()
            return
        g_near(zf, c, z).start()
        g_far(zf, c, z, 1 + at_end.astype(jnp.int32)).start()

    def forward_z(zf, c):
        if not tree:
            return

        @pl.when(in_middle)
        def _():
            g_far(zf, c, far[0], 1).wait_recv()
            g_far(zf, c, far[1], 2).wait_recv()
            g_two(zf, c).start()

    def gathered_z(zf, c):
        if not tree:
            for o in z_others:
                g_direct(zf, c, o, o).wait_recv()
            return
        g_near(zf, c, near).wait_recv()

        @pl.when(at_end)
        def _():
            g_two(zf, c).wait_recv()

    def spread_y(zf, c):
        y_part(zf, c, y).start()

    def gathered_y(zf, c):
        y_part(zf, c, 1 - y).wait_recv()

    def sum_core(c):
        core_rs(c).wait_recv()
        keep[c] += r_core[c].astype(jnp.float32)

    def spread_core(c):
        core_part(c, core).start()

    def down(c):
        slot = lax.rem(c, 2)
        down_copy(c, slot).wait()
        core_part(c, 1 - core).wait_recv()
        acc[...] += jnp.dot(gath[c, 0], wdb[slot, :half], preferred_element_type=jnp.float32)
        acc[...] += jnp.dot(gath[c, 1], wdb[slot, half:], preferred_element_type=jnp.float32)

        @pl.when(c + 2 < chunks)
        def _():
            down_copy(c + 2, slot).start()

    def both(*parts):
        def run(zf, c):
            for part in parts:
                part(zf, c)

        return run

    def plain(part):
        return lambda zf, c: part(c)

    y_first = [
        (13, both(gathered_y, plain(spread_core))),
        (11, both(gathered_z, spread_y)),
        (9, forward_z),
        (7, both(take_z, activate, spread_z)),
        (5, merge_z),
        (3, both(take_y, send_z)),
        (1, both(plain(sum_core), send_y)),
    ]
    z_first = [
        (13, both(gathered_z, plain(spread_core))),
        (11, forward_z),
        (9, both(gathered_y, spread_z)),
        (7, both(take_y, activate, spread_y)),
        (5, both(take_z, send_y)),
        (3, merge_z),
        (1, both(plain(sum_core), send_z)),
    ]
    def step(t, carry):
        @pl.when(t == 1)
        def _():
            sq_core().wait_recv()
            sq_s[1] = sq_s[0] + sq_r[0]
            sq_y().start()

        @pl.when(t == 2)
        def _():
            sq_y().wait_recv()
            sq_s[2] = sq_s[1] + sq_r[1]
            for o in z_others:
                sq_to(o).start()

        @pl.when(t == 3)
        def _():
            total = sq_s[2]
            for o in z_others:
                sq_from(o).wait_recv()
                total = total + sq_z[o]
            row_scale = lax.rsqrt(total / (depth * n) + 1e-06)
            scale[...] = jnp.broadcast_to(row_scale[:1], (128, batch)).T

        for first, second in zip(y_first, z_first):
            for zf, (offset, stage) in ((False, first), (True, second)):
                c = t - offset
                kind = (lax.rem(c, EVERY) == EVERY - 1) == zf

                @pl.when(jnp.logical_and(jnp.logical_and(c >= 0, c < chunks), kind))
                def _(c=c, stage=stage, zf=zf):
                    stage(zf, c)

        for offset, stage in ((0, up), (LAST, down)):
            c = t - offset

            @pl.when(jnp.logical_and(c >= 0, c < chunks))
            def _(c=c, stage=stage):
                stage(c)

        return carry

    lax.fori_loop(0, chunks + LAST, step, 0)

    out[...] = acc[...].astype(jnp.bfloat16)

    sq_core().wait_send()
    sq_y().wait_send()
    for o in z_others:
        sq_to(o).wait_send()

    def drain_kind(zf, c):
        y_rs(zf, c).wait_send()
        y_part(zf, c, y).wait_send()
        if not tree:
            for o in z_others:
                z_direct(zf, c, o, z).wait_send()
                g_direct(zf, c, o, z).wait_send()
            return

        @pl.when(at_end)
        def _():
            z_end(zf, c).wait_send()

        @pl.when(in_middle)
        def _():
            z_mid(zf, c).wait_send()
            z_merged(zf, c, 0).wait_send()
            z_merged(zf, c, 1).wait_send()
            g_two(zf, c).wait_send()

        g_near(zf, c, z).wait_send()
        g_far(zf, c, z, 1).wait_send()

    def drain(c, carry):
        core_rs(c).wait_send()
        core_part(c, core).wait_send()
        for zf in (False, True):

            @pl.when((lax.rem(c, EVERY) == EVERY - 1) == zf)
            def _(zf=zf):
                drain_kind(zf, c)

        return carry

    lax.fori_loop(0, chunks, drain, 0)


def local(n, activations, norm_gain, w_up, w_down):
    batch, depth = activations.shape
    width = w_up.shape[1]
    chunks = width // CHUNK
    half, rows, nz = CHUNK // 2, batch // 2, n // 4
    bf16, f32 = jnp.bfloat16, jnp.float32
    vmem, dma = pltpu.VMEM, pltpu.SemaphoreType.DMA
    in_vmem = pl.BlockSpec(memory_space=pltpu.VMEM)
    in_hbm = pl.BlockSpec(memory_space=pl.ANY)
    return pl.pallas_call(
        functools.partial(kernel, (n, depth, width, chunks)),
        out_shape=jax.ShapeDtypeStruct((batch, depth), bf16),
        in_specs=[in_vmem, in_vmem, in_hbm, in_hbm],
        out_specs=in_vmem,
        scratch_shapes=[
            vmem((batch, depth), bf16),
            vmem((batch, depth), f32),
            vmem((batch, 128), f32),
            vmem((2, 2, depth, half), bf16),
            vmem((2, CHUNK, depth), bf16),
            vmem((chunks, batch, half), f32),
            vmem((chunks, batch, half), bf16),
            vmem((chunks, batch, half), bf16),
            vmem((chunks, rows, half), bf16),
            vmem((chunks, rows, half), bf16),
            vmem((chunks, batch, half), bf16),
            vmem((chunks, batch, half), bf16),
            vmem((chunks, 2, batch // nz, half), bf16),
            vmem((chunks, 2, batch // nz, half), bf16),
            vmem((chunks, 2, batch, half), bf16),
            vmem((3, 8, batch), f32),
            vmem((2, 8, batch), f32),
            vmem((nz, 8, batch), f32),
            dma((2, 2)),
            dma((2,)),
            dma((chunks,)),
            dma((chunks,)),
            dma((chunks,)),
            dma((chunks,)),
            dma((chunks, nz)),
            dma((chunks, nz)),
            dma((chunks, nz)),
            dma((chunks, nz)),
            dma((chunks,)),
            dma((chunks,)),
            dma((chunks,)),
            dma((chunks,)),
            dma((2,)),
            dma((2,)),
            dma((nz,)),
            dma((nz,)),
        ],
        compiler_params=pltpu.CompilerParams(
            collective_id=0, has_side_effects=True, vmem_limit_bytes=60 * 1024 * 1024
        ),
        cost_estimate=pl.CostEstimate(
            flops=4 * batch * depth * width, bytes_accessed=4 * depth * width, transcendentals=batch * width // n
        ),
    )(activations, norm_gain[None, :], w_up, w_down)


def solution(mesh):
    return jax.shard_map(
        functools.partial(local, mesh.shape["gx"]),
        mesh=mesh,
        in_specs=(P("groups", "gx"), P("gx"), P("gx", None), P(None, "gx")),
        out_specs=P("groups", "gx"),
        check_vma=False,
    )
```
